512 devices in a mesh: seq: 64 (over x_lo, z, core), chan: 8 (over y, x_hi).
Axes of the slice: x: 4 (x_hi: 2, x_lo: 2; x = x_hi * 2 + x_lo), y: 4, z: 16, core: 2. Of those that a mesh axis runs over, the one named last changes fastest.
Arguments:
- query_proj: bfloat16 [8192, 4096], P('seq', 'chan'), may hold values from -6 to 6
- key_proj: bfloat16 [8192, 4096], P('seq', 'chan'), may hold values from -6 to 6
- value_proj: bfloat16 [8192, 4096], P('seq', 'chan'), may hold values from -6 to 6
- filter_taps: float32 [8192, 4096], P('seq', 'chan'), may hold values from -6 to 6
- skip_bias: float32 [4096], P('chan'), may hold values from -3 to 3
- out_weight: bfloat16 [4096, 4096], P('seq', 'chan'), may hold values from -0.09375 to 0.09375
Outputs:
- operator_out: bfloat16 [8192, 4096], P('seq', 'chan')
- convolved: float32 [8192, 4096], P('seq', 'chan')
The draws below stay inside these ranges and needn't reach their ends.
All inputs are finite; a program needn't handle non-finite values.
Results may differ from the reference program's by a relative error of at most 0.0049.
Values may be sent and summed in bfloat16 or wider, within the bound.
A program may use at most 64 MiB of HBM per device.

```python
import jax
import jax.numpy as jnp
from jax import lax

D = 4096
TOKENS = 8192
FFT_LEN = 16384
N_CHAN = 8


def shaped_taps(key, lower, upper):
    rate_key, noise_key = jax.random.split(key)
    unit = jax.random.uniform(rate_key, (1, D), jnp.float32)
    rates = jnp.exp(jnp.log(lower) + unit * (jnp.log(upper) - jnp.log(lower)))
    position = jnp.arange(TOKENS, dtype=jnp.int32).astype(jnp.float32)[:, None]
    envelope = jnp.exp(-rates * position)
    amplitude = jnp.sqrt(jnp.expm1(-2.0 * rates) / jnp.expm1(-2.0 * rates * TOKENS))
    noise = jax.random.truncated_normal(noise_key, -5.0, 5.0, (TOKENS, D), jnp.float32)
    return amplitude * envelope * noise


def draw_filter_taps(key, part):
    key = jax.random.fold_in(key, 11)
    head_key, floor_key, share_key = jax.random.split(key, 3)
    share = 0.1 + 0.2 * jax.random.uniform(share_key, (1, D), jnp.float32)
    floor = shaped_taps(floor_key, 0.25 / TOKENS, 2.0 / TOKENS)
    head = shaped_taps(head_key, 0.5 / TOKENS, 1.0 / 30.0)
    return jnp.sqrt(1.0 - share) * head + jnp.sqrt(share) * floor


def level_of(key, extent, shards, low, high):
    factor_of, own = 1.0, jax.random.fold_in(key, 6)
    for dim, shards_of in shards:
        draws = jnp.exp(jax.random.uniform(jax.random.fold_in(own, dim), (shards_of,), jnp.float32, low / len(shards), high / len(shards)))
        factor_of = factor_of * jnp.repeat(draws, extent[dim] // shards_of).reshape([-1 if axis == dim else 1 for axis in range(len(extent))])
    return factor_of


def scatter_about(rng, extent, scale, limit, cuts=(), kind=jnp.bfloat16):
    factor_of = level_of(rng, extent, cuts, -0.22, 0.18) if cuts else 1.0
    entries = jax.random.normal(rng, extent, jnp.float32) * scale * factor_of
    return jnp.minimum(jnp.maximum(entries, -limit), limit).astype(kind)


def setup_inputs(seed: int = 0) -> dict:
    key_list = jax.random.split(jax.random.key(seed), 7)
    query_proj = scatter_about(key_list[0], (TOKENS, D), 1.0, 6.0, ((0, 64), (1, 8)))
    key_proj = scatter_about(key_list[1], (TOKENS, D), 1.0, 6.0, ((0, 64), (1, 8)))
    value_proj = scatter_about(key_list[2], (TOKENS, D), 1.0, 6.0, ((0, 64), (1, 8)))
    filter_taps = draw_filter_taps(jax.random.fold_in(key_list[6], 71), 0)
    skip_bias = scatter_about(key_list[4], (D,), 1.0, 3.0, ((0, 8),), jnp.float32)
    out_weight = scatter_about(key_list[5], (D, D), D ** -0.5, 0.09375, ((0, 64), (1, 8)))
    return dict(query_proj=query_proj, key_proj=key_proj, value_proj=value_proj, filter_taps=filter_taps, skip_bias=skip_bias, out_weight=out_weight)


def reference(query_proj, key_proj, value_proj, filter_taps, skip_bias, out_weight):
    slab_width = D // N_CHAN

    def one_slab(group):
        offset = group * slab_width
        query_block = lax.dynamic_slice_in_dim(query_proj, offset, slab_width, 1)
        key_block = lax.dynamic_slice_in_dim(key_proj, offset, slab_width, 1)
        value_block = lax.dynamic_slice_in_dim(value_proj, offset, slab_width, 1)
        taps_block = lax.dynamic_slice_in_dim(filter_taps, offset, slab_width, 1)
        skip_block = lax.dynamic_slice_in_dim(skip_bias, offset, slab_width, 0)
        signal = key_block.astype(jnp.float32) * value_block.astype(jnp.float32)
        spectrum = jnp.fft.rfft(signal, n=FFT_LEN, axis=0) * jnp.fft.rfft(taps_block, n=FFT_LEN, axis=0)
        convolved = jnp.fft.irfft(spectrum, n=FFT_LEN, axis=0)[:TOKENS].astype(jnp.float32)
        mixed_sum = convolved + skip_block[None, :] * signal
        return (query_block.astype(jnp.float32) * mixed_sum).astype(jnp.bfloat16), convolved

    gated, convolved = lax.map(one_slab, jnp.arange(N_CHAN, dtype=jnp.int32))
    gated = jnp.transpose(gated, (1, 0, 2)).reshape(TOKENS, D)
    convolved = jnp.transpose(convolved, (1, 0, 2)).reshape(TOKENS, D)
    operator_out = jnp.dot(gated, out_weight, preferred_element_type=jnp.float32).astype(jnp.bfloat16)
    return (operator_out, convolved)
```

```python
import math

import jax
import jax.numpy as jnp
import numpy as np
from jax import lax
from jax.sharding import PartitionSpec as P

PRECISE = lax.Precision.HIGHEST


def tables(blocks, width):
    length = 2 * blocks * width
    half = np.arange(blocks) + 0.5
    angle = 2.0 * math.pi / (2 * blocks) * np.outer(half, np.arange(blocks))
    first = np.concatenate([np.cos(angle), -np.sin(angle)], axis=0)
    last = np.concatenate([np.cos(angle), -np.sin(angle)], axis=0).T * (2.0 / length)
    twist = 2.0 * math.pi / length * np.outer(half, np.arange(width))
    second = 2.0 * math.pi / width * (np.outer(np.arange(width), np.arange(width)) % width)
    c, s = np.cos(second), np.sin(second)
    forward = np.block([[c, -s], [s, c]])
    backward = np.block([[c, s], [-s, c]])
    f32 = lambda a: a.astype(np.float32)
    return f32(first), f32(last), f32(np.cos(twist)), f32(np.sin(twist)), f32(forward), f32(backward)


def body(query_proj, key_proj, value_proj, filter_taps, skip_bias, out_weight):
    tok_rows, slab_width = query_proj.shape
    shards = lax.axis_size("seq")
    own = slab_width // shards
    first, last, tw_cos, tw_sin, forward, backward = tables(shards, tok_rows)
    signal = key_proj.astype(jnp.float32) * value_proj.astype(jnp.float32)
    outgoing = jnp.concatenate(
        [
            signal.astype(jnp.bfloat16).T.reshape(shards, own, tok_rows),
            filter_taps.astype(jnp.bfloat16).T.reshape(shards, own, tok_rows),
        ],
        axis=1,
    )
    arrived = lax.all_to_all(outgoing, "seq", split_axis=0, concat_axis=0, tiled=True)
    arrived = arrived.astype(jnp.float32)
    mixed = jnp.einsum("ka,acb->kcb", first, arrived, precision=PRECISE)
    re, im = mixed[:shards], mixed[shards:]
    wc, ws = tw_cos[:, None, :], tw_sin[:, None, :]
    turned = jnp.concatenate([re * wc + im * ws, im * wc - re * ws], axis=-1)
    freq = jnp.einsum("kcb,bf->kcf", turned, forward, precision=PRECISE)
    fr, fi = freq[..., :tok_rows], freq[..., tok_rows:]
    sr, si, hr, hi = fr[:, :own], fi[:, :own], fr[:, own:], fi[:, own:]
    prod = jnp.concatenate([sr * hr - si * hi, sr * hi + si * hr], axis=-1)
    back = jnp.einsum("kcf,fb->kcb", prod, backward, precision=PRECISE)
    br, bi = back[..., :tok_rows], back[..., tok_rows:]
    unturned = jnp.concatenate([br * wc - bi * ws, bi * wc + br * ws], axis=0)
    conv = jnp.einsum("ak,kcb->acb", last, unturned, precision=PRECISE)
    home = lax.all_to_all(conv.astype(jnp.bfloat16), "seq", split_axis=0, concat_axis=0, tiled=True)
    convolved = home.reshape(slab_width, tok_rows).T.astype(jnp.float32)
    mixed_sum = convolved + skip_bias[None, :] * signal
    gated = (query_proj.astype(jnp.float32) * mixed_sum).astype(jnp.bfloat16)
    whole = lax.all_gather(gated, "chan", axis=1, tiled=True)
    result = jnp.dot(
        whole,
        lax.all_gather(out_weight, "seq", axis=0, tiled=True),
        preferred_element_type=jnp.float32,
    )
    return (result.astype(jnp.bfloat16), convolved)


def solution(mesh):
    return jax.shard_map(
        body,
        mesh=mesh,
        in_specs=(
            P("seq", "chan"),
            P("seq", "chan"),
            P("seq", "chan"),
            P("seq", "chan"),
            P("chan"),
            P("seq", "chan"),
        ),
        out_specs=(P("seq", "chan"), P("seq", "chan")),
        check_vma=False,
    )
```

```python
import functools
import math

import jax
import jax.numpy as jnp
import ml_dtypes
import numpy as np
from jax import lax
from jax.experimental import pallas as pl
from jax.experimental.pallas import tpu as pltpu
from jax.sharding import PartitionSpec as P

MESH = pl.DeviceIdType.MESH
BF16 = jnp.bfloat16
F32 = jnp.float32

SEQ = 64
ZLEN = 16
CHAN = 8
ROWS = 128
SLAB = 512
OWN = 8
WROWS = 64


def split(a):
    hi = a.astype(ml_dtypes.bfloat16)
    lo = (a - hi.astype(np.float64)).astype(ml_dtypes.bfloat16)
    return hi, lo


def tables():
    length = 2 * SEQ * ROWS
    half = np.arange(SEQ) + 0.5
    angle = 2.0 * math.pi / (2 * SEQ) * np.outer(half, np.arange(SEQ))
    first = np.concatenate([np.cos(angle), -np.sin(angle)], axis=0)
    last = first.T * (2.0 / length)
    twist = 2.0 * math.pi / length * np.outer(half, np.arange(ROWS))
    second = 2.0 * math.pi / ROWS * (np.outer(np.arange(ROWS), np.arange(ROWS)) % ROWS)
    c, s = np.cos(second), np.sin(second)
    forward = np.block([[c, -s], [s, c]])
    backward = np.block([[c, s], [-s, c]])
    f_hi, f_lo = split(first)
    l_hi, l_lo = split(last)
    w_hi, w_lo = split(forward)
    b_hi, b_lo = split(backward)
    return (
        np.concatenate([f_hi, f_lo], axis=1),
        np.stack([w_hi, w_lo, b_hi, b_lo]),
        np.concatenate([l_hi, l_lo, l_hi], axis=1),
        np.stack([np.cos(twist), np.sin(twist)]).astype(np.float32),
    )


def dot(a, b):
    return jnp.dot(a, b, preferred_element_type=F32)


def halves(a):
    hi = a.astype(BF16)
    return hi, (a - hi.astype(F32)).astype(BF16)


def kernel(
    q_ref, k_ref, v_ref, t_ref, skip_ref, w_ref, first_ref, second_ref, last_ref, twist_ref,
    out_ref, conv_ref,
    send_in, recv_in, send_back, recv_back, wide, freq, spread_hi, spread_lo, back_f, gated, weight,
    in_s, in_r, back_s, back_r, local, up_s, up_r, down_s, down_r, x_s, x_r, core_s, core_r, core2_s, core2_r,
    ga_s, ga_r,
):
    me = lax.axis_index("seq")
    slab = lax.axis_index("chan")
    x_lo, z, core = me // 32, (me % 32) // 2, me % 2
    y, x_hi = slab // 2, slab % 2
    ring = x_lo * 2 + core
    up = x_lo * 32 + ((z + 1) % ZLEN) * 2 + core
    down = x_lo * 32 + ((z + ZLEN - 1) % ZLEN) * 2 + core
    across = (1 - x_lo) * 32 + z * 2 + core
    twin = x_lo * 32 + z * 2 + (1 - core)

    def remote(src, dst, ss, rs, **where):
        return pltpu.make_async_remote_copy(
            src_ref=src, dst_ref=dst, send_sem=ss, recv_sem=rs, device_id=where, device_id_type=MESH
        )

    barrier = pltpu.get_barrier_semaphore()

    def greet(off, carry):
        pl.semaphore_signal(barrier, inc=1, device_id={"seq": (me + off) % SEQ}, device_id_type=MESH)
        return carry

    lax.fori_loop(1, SEQ, greet, 0)
    column = [((y + dy) % 4) * 2 + x_hi for dy in (1, 3, 2)]
    beside = y * 2 + (1 - x_hi)
    for other in column + [beside]:
        pl.semaphore_signal(barrier, inc=1, device_id={"chan": other}, device_id_type=MESH)

    signal = k_ref[...].astype(F32) * v_ref[...].astype(F32)
    send_in[...] = jnp.concatenate(
        [signal.T.reshape(SEQ, OWN, ROWS), t_ref[...].T.reshape(SEQ, OWN, ROWS)], axis=1
    ).astype(BF16)
    weight[ring, 0] = w_ref[...]

    pl.semaphore_wait(barrier, SEQ - 1 + 4)

    def exchange(source, target, ss, rs):
        def some(i, carry):
            step = 8 - (i + 1) // 2
            dz = jnp.where(i % 2 == 0, step, ZLEN - step) % ZLEN
            for dx in (0, 1):
                for dc in (0, 1):
                    there = ((x_lo + dx) % 2) * 32 + ((z + dz) % ZLEN) * 2 + (core + dc) % 2
                    remote(source.at[there], target.at[me], ss, rs, seq=there).start()
            return carry

        lax.fori_loop(0, 15, some, 0)
        for dx, dc in ((1, 0), (1, 1), (0, 1)):
            there = ((x_lo + dx) % 2) * 32 + z * 2 + (core + dc) % 2
            remote(source.at[there], target.at[me], ss, rs, seq=there).start()
        own = pltpu.make_async_copy(source.at[me], target.at[me], local)
        own.start()
        own.wait()

    def drain(buffer, sem):
        view = buffer.at[pl.ds(0, SEQ - 1)]
        pltpu.make_async_copy(view, view, sem).wait()

    def up_copy(t):
        return remote(weight.at[ring, (ZLEN - t) % ZLEN], weight.at[ring, 15 - t], up_s.at[t], up_r.at[t], seq=up)

    def down_copy(t):
        return remote(weight.at[ring, t], weight.at[ring, t + 1], down_s.at[t], down_r.at[t], seq=down)

    other_ring = (1 - x_lo) * 2 + core

    def part(r, i):
        return weight.at[r, pl.ds(4 * i, 4)]

    def x_copy(i):
        return remote(part(ring, i), part(ring, i), x_s.at[i], x_r.at[i], seq=across)

    def core_copy(i):
        return remote(part(ring, i), part(ring, i), core_s.at[i], core_r.at[i], seq=twin)

    def core2_copy(i):
        return remote(part(other_ring, i), part(other_ring, i), core2_s.at[i], core2_r.at[i], seq=twin)

    def ring_step(t):
        up_copy(t).wait_recv()
        if t < 7:
            up_copy(t + 1).start()
            down_copy(t).wait_recv()
            if t < 6:
                down_copy(t + 1).start()
        done = {2: 0, 3: 3, 6: 1, 7: 2}.get(t)
        if done is not None:
            x_copy(done).start()
            core_copy(done).start()

    def pass_on(i):
        x_copy(i).wait_recv()
        core2_copy(i).start()

    exchange(send_in, recv_in, in_s, in_r)
    up_copy(0).start()
    down_copy(0).start()
    for t in range(4):
        ring_step(t)
    drain(recv_in, in_r)

    wide[...] = recv_in[...].astype(F32).reshape(SEQ * 16, ROWS)
    stacked = jnp.concatenate([wide[pl.ds(c, SEQ, stride=16), :] for c in range(16)], axis=1).astype(BF16)
    freq[...] = dot(first_ref[...], jnp.concatenate([stacked, stacked], axis=0))
    cos, sin = twist_ref[0], twist_ref[1]
    for c in range(16):
        cols = pl.ds(c * ROWS, ROWS)
        rows = pl.ds(c * SEQ, SEQ)
        re, im = freq[0:SEQ, cols], freq[SEQ : 2 * SEQ, cols]
        turned = jnp.concatenate([re * cos + im * sin, im * cos - re * sin], axis=1)
        spread_hi[rows, :], spread_lo[rows, :] = halves(turned)
    ring_step(4)
    hi, lo = spread_hi[...], spread_lo[...]
    spec = dot(hi, second_ref[0]) + dot(lo, second_ref[0]) + dot(hi, second_ref[1])
    n = OWN * SEQ
    sr, si, hr, hi_ = spec[:n, :ROWS], spec[:n, ROWS:], spec[n:, :ROWS], spec[n:, ROWS:]
    prod = jnp.concatenate([sr * hr - si * hi_, sr * hi_ + si * hr], axis=1)
    hi, lo = halves(prod)
    back = dot(hi, second_ref[2]) + dot(lo, second_ref[2]) + dot(hi, second_ref[3])
    ring_step(5)
    pieces_hi, pieces_lo = [], []
    for c in range(OWN):
        re, im = back[c * SEQ : (c + 1) * SEQ, :ROWS], back[c * SEQ : (c + 1) * SEQ, ROWS:]
        unturned = jnp.concatenate([re * cos - im * sin, im * cos + re * sin], axis=0)
        hi, lo = halves(unturned)
        pieces_hi.append(hi)
        pieces_lo.append(lo)
    u_hi, u_lo = jnp.concatenate(pieces_hi, axis=1), jnp.concatenate(pieces_lo, axis=1)
    done = dot(last_ref[...], jnp.concatenate([u_hi, u_hi, u_lo], axis=0))
    for c in range(OWN):
        back_f[pl.ds(c, SEQ, stride=OWN), :] = done[:, c * ROWS : (c + 1) * ROWS]
    send_back[...] = back_f[...].reshape(SEQ, OWN, ROWS).astype(BF16)

    exchange(send_back, recv_back, back_s, back_r)
    ring_step(6)
    ring_step(7)
    pass_on(0)
    pass_on(3)
    drain(recv_back, back_r)

    convolved = recv_back[...].astype(F32).reshape(SLAB, ROWS).T
    conv_ref[...] = convolved
    signal = k_ref[...].astype(F32) * v_ref[...].astype(F32)
    gated[slab] = (q_ref[...].astype(F32) * (convolved + skip_ref[...] * signal)).astype(BF16)

    def g_copy(source, i, other):
        return remote(gated.at[source], gated.at[source], ga_s.at[i], ga_r.at[i], chan=other)

    sends = [g_copy(slab, 3, beside)] + [g_copy(slab, i, column[i]) for i in range(3)]
    for copy in sends:
        copy.start()
    g_copy(beside, 3, beside).wait_recv()
    more = [g_copy(beside, 4 + i, column[i]) for i in range(3)]
    for copy in more:
        copy.start()
    pass_on(1)
    pass_on(2)
    for i in range(4):
        core_copy(i).wait_recv()
        core2_copy(i).wait_recv()

    def term(source):
        blocks = []
        for j in range(4):
            rel = (4 * (source % 4) + j + ZLEN - z) % ZLEN
            for half in (0, 1):
                blocks.append(weight[(source // 4) * 2 + half, rel])
        return dot(gated[source], jnp.concatenate(blocks, axis=0))

    total = term(slab) + term(beside)
    for base, flip in ((0, False), (4, True)):
        for i, dy in enumerate((3, 1, 2)):
            source = ((y + dy) % 4) * 2 + (1 - x_hi if flip else x_hi)
            g_copy(source, base + i, column[i]).wait_recv()
            total = total + term(source)
    out_ref[...] = total.astype(BF16)

    drain(send_in, in_s)
    drain(send_back, back_s)
    for t in range(8):
        up_copy(t).wait_send()
        if t < 7:
            down_copy(t).wait_send()
    for i in range(4):
        x_copy(i).wait_send()
        core_copy(i).wait_send()
        core2_copy(i).wait_send()
    for copy in sends + more:
        copy.wait_send()


def body(query_proj, key_proj, value_proj, filter_taps, skip_bias, out_weight):
    dma = pltpu.SemaphoreType.DMA
    vmem = pl.BlockSpec(memory_space=pltpu.VMEM)
    consts = [jnp.asarray(t) for t in tables()]
    return pl.pallas_call(
        kernel,
        out_shape=(
            jax.ShapeDtypeStruct((ROWS, SLAB), BF16),
            jax.ShapeDtypeStruct((ROWS, SLAB), F32),
        ),
        in_specs=[vmem] * 10,
        out_specs=(vmem, vmem),
        scratch_shapes=[
            pltpu.VMEM((SEQ, 16, ROWS), BF16),
            pltpu.VMEM((SEQ, 16, ROWS), BF16),
            pltpu.VMEM((SEQ, OWN, ROWS), BF16),
            pltpu.VMEM((SEQ, OWN, ROWS), BF16),
            pltpu.VMEM((SEQ * 16, ROWS), F32),
            pltpu.VMEM((2 * SEQ, 16 * ROWS), F32),
            pltpu.VMEM((16 * SEQ, 2 * ROWS), BF16),
            pltpu.VMEM((16 * SEQ, 2 * ROWS), BF16),
            pltpu.VMEM((SEQ * OWN, ROWS), F32),
            pltpu.VMEM((CHAN, ROWS, SLAB), BF16),
            pltpu.VMEM((4, ZLEN, WROWS, SLAB), BF16),
            dma, dma, dma, dma, dma,
            dma((8,)), dma((8,)), dma((7,)), dma((7,)),
            dma((4,)), dma((4,)), dma((4,)), dma((4,)), dma((4,)), dma((4,)),
            dma((7,)), dma((7,)),
        ],
        compiler_params=pltpu.CompilerParams(
            collective_id=0, has_side_effects=True, vmem_limit_bytes=48 * 1024 * 1024
        ),
        name="hyena",
    )(query_proj, key_proj, value_proj, filter_taps, skip_bias.reshape(1, SLAB), out_weight, *consts)


def solution(mesh):
    return jax.shard_map(
        body,
        mesh=mesh,
        in_specs=(
            P("seq", "chan"),
            P("seq", "chan"),
            P("seq", "chan"),
            P("seq", "chan"),
            P("chan"),
            P("seq", "chan"),
        ),
        out_specs=(P("seq", "chan"), P("seq", "chan")),
        check_vma=False,
    )
```

```python
import functools
import math

import jax
import jax.numpy as jnp
import ml_dtypes
import numpy as np
from jax import lax
from jax.experimental import pallas as pl
from jax.experimental.pallas import tpu as pltpu
from jax.sharding import PartitionSpec as P

MESH = pl.DeviceIdType.MESH
BF16 = jnp.bfloat16
F32 = jnp.float32

SEQ = 64
ZLEN = 16
CHAN = 8
ROWS = 128
SLAB = 512
OWN = 8
WROWS = 64
PAIRS = (0, 14, 2, 12, 4, 10, 6, 8)


def split(a):
    hi = a.astype(ml_dtypes.bfloat16)
    lo = (a - hi.astype(np.float64)).astype(ml_dtypes.bfloat16)
    return hi, lo


def tables():
    length = 2 * SEQ * ROWS
    half = np.arange(SEQ) + 0.5
    angle = 2.0 * math.pi / (2 * SEQ) * np.outer(half, np.arange(SEQ))
    first = np.concatenate([np.cos(angle), -np.sin(angle)], axis=0)
    last = first.T * (2.0 / length)
    twist = 2.0 * math.pi / length * np.outer(half, np.arange(ROWS))
    second = 2.0 * math.pi / ROWS * (np.outer(np.arange(ROWS), np.arange(ROWS)) % ROWS)
    c, s = np.cos(second), np.sin(second)
    forward = np.block([[c, -s], [s, c]])
    backward = np.block([[c, s], [-s, c]])
    f_hi, f_lo = split(first)
    l_hi, l_lo = split(last)
    return tuple(
        table.astype(np.float32)
        for table in (
            np.concatenate([f_hi, f_lo], axis=1),
            np.stack([forward, backward]),
            np.concatenate([l_hi, l_lo, l_hi], axis=1),
            np.stack([np.cos(twist), np.sin(twist)]),
        )
    )


def dot(a, b):
    return jnp.dot(a, b, preferred_element_type=F32)


def halves(a):
    hi = a.astype(BF16)
    return hi, (a - hi.astype(F32)).astype(BF16)


def kernel(
    q_hbm, k_hbm, v_hbm, t_hbm, skip_hbm, w_hbm, first_hbm, second_hbm, last_hbm, twist_hbm,
    out_ref, conv_ref,
    q_ref, k_ref, v_ref, t_ref, skip_ref, w_ref, first_f, second_f, last_f, twist_ref,
    first_ref, second_ref, last_ref,
    send_t, recv_t, send_s, recv_s, send_back, recv_back, wide, freq, spread_hi, spread_lo, taps_spec, gated, weight,
    int_s, int_r, ins_s, ins_r, back_s, back_r, local, up_s, up_r, down_s, down_r, x_s, x_r, core_s, core_r, core2_s, core2_r,
    ga_s, ga_r, fetch_s,
):
    me = lax.axis_index("seq")
    slab = lax.axis_index("chan")
    x_lo, z, core = me // 32, (me % 32) // 2, me % 2
    y, x_hi = slab // 2, slab % 2
    ring = x_lo * 2 + core
    up = x_lo * 32 + ((z + 1) % ZLEN) * 2 + core
    down = x_lo * 32 + ((z + ZLEN - 1) % ZLEN) * 2 + core
    across = (1 - x_lo) * 32 + z * 2 + core
    twin = x_lo * 32 + z * 2 + (1 - core)

    def remote(src, dst, ss, rs, **where):
        return pltpu.make_async_remote_copy(
            src_ref=src, dst_ref=dst, send_sem=ss, recv_sem=rs, device_id=where, device_id_type=MESH
        )

    fetches = [
        pltpu.make_async_copy(src, dst, fetch_s.at[i])
        for i, (src, dst) in enumerate(
            [
                (t_hbm, t_ref), (w_hbm, w_ref), (k_hbm, k_ref), (v_hbm, v_ref), (first_hbm, first_f),
                (second_hbm, second_f), (last_hbm, last_f), (twist_hbm, twist_ref), (q_hbm, q_ref), (skip_hbm, skip_ref),
            ]
        )
    ]
    for fetch in fetches:
        fetch.start()

    barrier = pltpu.get_barrier_semaphore()

    def greet(off, carry):
        pl.semaphore_signal(barrier, inc=1, device_id={"seq": (me + off) % SEQ}, device_id_type=MESH)
        return carry

    lax.fori_loop(1, SEQ, greet, 0)
    column = [((y + dy) % 4) * 2 + x_hi for dy in (1, 3, 2)]
    beside = y * 2 + (1 - x_hi)
    for other in column + [beside]:
        pl.semaphore_signal(barrier, inc=1, device_id={"chan": other}, device_id_type=MESH)

    for fetch in fetches[:2]:
        fetch.wait()
    send_t[...] = t_ref[...].T.reshape(SEQ, OWN, ROWS).astype(BF16)
    weight[ring, 0] = w_ref[...]
    pl.semaphore_wait(barrier, SEQ - 1 + 4)

    def exchange(source, target, ss, rs):
        def some(i, carry):
            step = 8 - (i + 1) // 2
            dz = jnp.where(i % 2 == 0, step, ZLEN - step) % ZLEN
            for dx in (0, 1):
                for dc in (0, 1):
                    there = ((x_lo + dx) % 2) * 32 + ((z + dz) % ZLEN) * 2 + (core + dc) % 2
                    remote(source.at[there], target.at[me], ss, rs, seq=there).start()
            return carry

        lax.fori_loop(0, 15, some, 0)
        for dx, dc in ((1, 0), (1, 1), (0, 1)):
            there = ((x_lo + dx) % 2) * 32 + z * 2 + (core + dc) % 2
            remote(source.at[there], target.at[me], ss, rs, seq=there).start()
        own = pltpu.make_async_copy(source.at[me], target.at[me], local)
        own.start()
        own.wait()

    def drain(buffer, sem):
        view = buffer.at[pl.ds(0, SEQ - 1)]
        pltpu.make_async_copy(view, view, sem).wait()

    def up_copy(t):
        return remote(weight.at[ring, (ZLEN - t) % ZLEN], weight.at[ring, 15 - t], up_s.at[t], up_r.at[t], seq=up)

    def down_copy(t):
        return remote(weight.at[ring, t], weight.at[ring, t + 1], down_s.at[t], down_r.at[t], seq=down)

    other_ring = (1 - x_lo) * 2 + core

    def part(r, i):
        return weight.at[r, pl.ds(PAIRS[i], 2)]

    def x_copy(i):
        return remote(part(ring, i), part(ring, i), x_s.at[i], x_r.at[i], seq=across)

    def core_copy(i):
        return remote(part(ring, i), part(ring, i), core_s.at[i], core_r.at[i], seq=twin)

    def core2_copy(i):
        return remote(part(other_ring, i), part(other_ring, i), core2_s.at[i], core2_r.at[i], seq=twin)

    def ring_step(t):
        up_copy(t).wait_recv()
        if t < 7:
            up_copy(t + 1).start()
            down_copy(t).wait_recv()
            if t < 6:
                down_copy(t + 1).start()
        x_copy(t).start()
        core_copy(t).start()

    def pass_on(i):
        x_copy(i).wait_recv()
        core2_copy(i).start()

    up_copy(0).start()
    down_copy(0).start()
    exchange(send_t, recv_t, int_s, int_r)
    for fetch in fetches[2:4]:
        fetch.wait()
    signal = k_ref[...].astype(F32) * v_ref[...].astype(F32)
    send_s[...] = signal.T.reshape(SEQ, OWN, ROWS).astype(BF16)
    ring_step(0)
    exchange(send_s, recv_s, ins_s, ins_r)
    for fetch in fetches[4:]:
        fetch.wait()
    first_ref[...] = first_f[...].astype(BF16)
    last_ref[...] = last_f[...].astype(BF16)
    for i in range(2):
        second_ref[2 * i], second_ref[2 * i + 1] = halves(second_f[i])
    cos, sin = twist_ref[0], twist_ref[1]

    def transform(arrived):
        wide[...] = arrived[...].astype(F32).reshape(SEQ * OWN, ROWS)
        stacked = jnp.concatenate([wide[pl.ds(c, SEQ, stride=OWN), :] for c in range(OWN)], axis=1).astype(BF16)
        freq[...] = dot(first_ref[...], jnp.concatenate([stacked, stacked], axis=0))
        for c in range(OWN):
            cols = pl.ds(c * ROWS, ROWS)
            rows = pl.ds(c * SEQ, SEQ)
            re, im = freq[0:SEQ, cols], freq[SEQ : 2 * SEQ, cols]
            turned = jnp.concatenate([re * cos + im * sin, im * cos - re * sin], axis=1)
            spread_hi[rows, :], spread_lo[rows, :] = halves(turned)
        hi, lo = spread_hi[...], spread_lo[...]
        return dot(hi, second_ref[0]) + dot(lo, second_ref[0]) + dot(hi, second_ref[1])

    drain(recv_t, int_r)
    taps_spec[...] = transform(recv_t)
    ring_step(1)
    drain(recv_s, ins_r)
    spec = transform(recv_s)
    ring_step(2)
    pass_on(0)
    sr, si, hr, hi_ = spec[:, :ROWS], spec[:, ROWS:], taps_spec[:, :ROWS], taps_spec[:, ROWS:]
    prod = jnp.concatenate([sr * hr - si * hi_, sr * hi_ + si * hr], axis=1)
    hi, lo = halves(prod)
    back = dot(hi, second_ref[2]) + dot(lo, second_ref[2]) + dot(hi, second_ref[3])
    ring_step(3)
    pass_on(1)
    pieces_hi, pieces_lo = [], []
    for c in range(OWN):
        re, im = back[c * SEQ : (c + 1) * SEQ, :ROWS], back[c * SEQ : (c + 1) * SEQ, ROWS:]
        unturned = jnp.concatenate([re * cos - im * sin, im * cos + re * sin], axis=0)
        hi, lo = halves(unturned)
        pieces_hi.append(hi)
        pieces_lo.append(lo)
    u_hi, u_lo = jnp.concatenate(pieces_hi, axis=1), jnp.concatenate(pieces_lo, axis=1)
    done = dot(last_ref[...], jnp.concatenate([u_hi, u_hi, u_lo], axis=0))
    for c in range(OWN):
        wide[pl.ds(c, SEQ, stride=OWN), :] = done[:, c * ROWS : (c + 1) * ROWS]
    send_back[...] = wide[...].reshape(SEQ, OWN, ROWS).astype(BF16)

    exchange(send_back, recv_back, back_s, back_r)
    ring_step(4)
    pass_on(2)
    drain(recv_back, back_r)
    ring_step(5)
    pass_on(3)

    convolved = recv_back[...].astype(F32).reshape(SLAB, ROWS).T
    conv_ref[...] = convolved
    signal = k_ref[...].astype(F32) * v_ref[...].astype(F32)
    gated[slab] = (q_ref[...].astype(F32) * (convolved + skip_ref[...][None, :] * signal)).astype(BF16)

    def g_copy(source, i, other):
        return remote(gated.at[source], gated.at[source], ga_s.at[i], ga_r.at[i], chan=other)

    sends = [g_copy(slab, 3, beside)] + [g_copy(slab, i, column[i]) for i in range(3)]
    for copy in sends:
        copy.start()
    ring_step(6)
    pass_on(4)
    g_copy(beside, 3, beside).wait_recv()
    more = [g_copy(beside, 4 + i, column[i]) for i in range(3)]
    for copy in more:
        copy.start()
    ring_step(7)
    for i in (5, 6, 7):
        pass_on(i)
    for i in range(8):
        core_copy(i).wait_recv()
        core2_copy(i).wait_recv()

    def term(source):
        blocks = []
        for j in range(4):
            rel = (4 * (source % 4) + j + ZLEN - z) % ZLEN
            for half in (0, 1):
                blocks.append(weight[(source // 4) * 2 + half, rel])
        return dot(gated[source], jnp.concatenate(blocks, axis=0))

    total = term(slab) + term(beside)
    for base, flip in ((0, False), (4, True)):
        for i, dy in enumerate((3, 1, 2)):
            source = ((y + dy) % 4) * 2 + (1 - x_hi if flip else x_hi)
            g_copy(source, base + i, column[i]).wait_recv()
            total = total + term(source)
    out_ref[...] = total.astype(BF16)

    drain(send_t, int_s)
    drain(send_s, ins_s)
    drain(send_back, back_s)
    for t in range(8):
        up_copy(t).wait_send()
        if t < 7:
            down_copy(t).wait_send()
    for i in range(8):
        x_copy(i).wait_send()
        core_copy(i).wait_send()
        core2_copy(i).wait_send()
    for copy in sends + more:
        copy.wait_send()


def body(query_proj, key_proj, value_proj, filter_taps, skip_bias, out_weight):
    dma = pltpu.SemaphoreType.DMA
    vmem = pl.BlockSpec(memory_space=pltpu.VMEM)
    consts = [jnp.asarray(t) for t in tables()]
    return pl.pallas_call(
        kernel,
        out_shape=(
            jax.ShapeDtypeStruct((ROWS, SLAB), BF16),
            jax.ShapeDtypeStruct((ROWS, SLAB), F32),
        ),
        in_specs=[pl.BlockSpec(memory_space=pltpu.HBM)] * 10,
        out_specs=(vmem, vmem),
        scratch_shapes=[
            pltpu.VMEM((ROWS, SLAB), BF16),
            pltpu.VMEM((ROWS, SLAB), BF16),
            pltpu.VMEM((ROWS, SLAB), BF16),
            pltpu.VMEM((ROWS, SLAB), F32),
            pltpu.VMEM((SLAB,), F32),
            pltpu.VMEM((WROWS, SLAB), BF16),
            pltpu.VMEM((2 * SEQ, 2 * SEQ), F32),
            pltpu.VMEM((2, 2 * ROWS, 2 * ROWS), F32),
            pltpu.VMEM((SEQ, 6 * SEQ), F32),
            pltpu.VMEM((2, SEQ, ROWS), F32),
            pltpu.VMEM((2 * SEQ, 2 * SEQ), BF16),
            pltpu.VMEM((4, 2 * ROWS, 2 * ROWS), BF16),
            pltpu.VMEM((SEQ, 6 * SEQ), BF16),
            pltpu.VMEM((SEQ, OWN, ROWS), BF16),
            pltpu.VMEM((SEQ, OWN, ROWS), BF16),
            pltpu.VMEM((SEQ, OWN, ROWS), BF16),
            pltpu.VMEM((SEQ, OWN, ROWS), BF16),
            pltpu.VMEM((SEQ, OWN, ROWS), BF16),
            pltpu.VMEM((SEQ, OWN, ROWS), BF16),
            pltpu.VMEM((SEQ * OWN, ROWS), F32),
            pltpu.VMEM((2 * SEQ, OWN * ROWS), F32),
            pltpu.VMEM((OWN * SEQ, 2 * ROWS), BF16),
            pltpu.VMEM((OWN * SEQ, 2 * ROWS), BF16),
            pltpu.VMEM((OWN * SEQ, 2 * ROWS), F32),
            pltpu.VMEM((CHAN, ROWS, SLAB), BF16),
            pltpu.VMEM((4, ZLEN, WROWS, SLAB), BF16),
            dma, dma, dma, dma, dma, dma, dma,
            dma((8,)), dma((8,)), dma((7,)), dma((7,)),
            dma((8,)), dma((8,)), dma((8,)), dma((8,)), dma((8,)), dma((8,)),
            dma((7,)), dma((7,)), dma((10,)),
        ],
        compiler_params=pltpu.CompilerParams(
            collective_id=0, has_side_effects=True, vmem_limit_bytes=63 * 1024 * 1024
        ),
        name="hyena",
    )(query_proj, key_proj, value_proj, filter_taps, skip_bias, out_weight, *consts)


def solution(mesh):
    return jax.shard_map(
        body,
        mesh=mesh,
        in_specs=(
            P("seq", "chan"),
            P("seq", "chan"),
            P("seq", "chan"),
            P("seq", "chan"),
            P("chan"),
            P("seq", "chan"),
        ),
        out_specs=(P("seq", "chan"), P("seq", "chan")),
        check_vma=False,
    )
```

```python
import functools
import math

import jax
import jax.numpy as jnp
import ml_dtypes
import numpy as np
from jax import lax
from jax.experimental import pallas as pl
from jax.experimental.pallas import tpu as pltpu
from jax.sharding import PartitionSpec as P

MESH = pl.DeviceIdType.MESH
BF16 = jnp.bfloat16
F32 = jnp.float32

SEQ = 64
ZLEN = 16
CHAN = 8
ROWS = 128
SLAB = 512
OWN = 8
WROWS = 64
PAIRS = (0, 14, 2, 12, 4, 10, 6, 8)


def split(a):
    hi = a.astype(ml_dtypes.bfloat16)
    lo = (a - hi.astype(np.float64)).astype(ml_dtypes.bfloat16)
    return hi, lo


def tables():
    length = 2 * SEQ * ROWS
    half = np.arange(SEQ) + 0.5
    angle = 2.0 * math.pi / (2 * SEQ) * np.outer(half, np.arange(SEQ))
    first = np.concatenate([np.cos(angle), -np.sin(angle)], axis=0)
    last = first.T * (2.0 / length)
    twist = 2.0 * math.pi / length * np.outer(half, np.arange(ROWS))
    second = 2.0 * math.pi / ROWS * (np.outer(np.arange(ROWS), np.arange(ROWS)) % ROWS)
    c, s = np.cos(second), np.sin(second)
    forward = np.block([[c, -s], [s, c]])
    backward = np.block([[c, s], [-s, c]])
    f_hi, f_lo = split(first)
    l_hi, l_lo = split(last)
    return tuple(
        table.astype(np.float32)
        for table in (
            np.concatenate([f_hi, f_lo], axis=1),
            np.stack([forward, backward]),
            np.concatenate([l_hi, l_lo, l_hi], axis=1),
            np.stack([np.cos(twist), np.sin(twist)]),
        )
    )


def dot(a, b):
    return jnp.dot(a, b, preferred_element_type=F32)


def halves(a):
    hi = a.astype(BF16)
    return hi, (a - hi.astype(F32)).astype(BF16)


def kernel(
    q_hbm, k_hbm, v_hbm, t_hbm, skip_hbm, w_hbm, first_hbm, second_hbm, last_hbm, twist_hbm,
    out_ref, conv_ref,
    q_ref, k_ref, v_ref, t_ref, skip_ref, w_ref, first_f, second_f, last_f, twist_ref,
    first_ref, second_ref, last_ref,
    send_in, recv_in, send_back, recv_back, wide, freq, spread_hi, spread_lo, back_f, gated, weight,
    in_s, in_r, back_s, back_r, up_s, up_r, down_s, down_r, x_s, x_r, core_s, core_r, core2_s, core2_r,
    far_s, far_r,
    ga_s, ga_r, fetch_s,
):
    me = lax.axis_index("seq")
    slab = lax.axis_index("chan")
    x_lo, z, core = me // 32, (me % 32) // 2, me % 2
    y, x_hi = slab // 2, slab % 2
    ring = x_lo * 2 + core
    up = x_lo * 32 + ((z + 1) % ZLEN) * 2 + core
    down = x_lo * 32 + ((z + ZLEN - 1) % ZLEN) * 2 + core
    across = (1 - x_lo) * 32 + z * 2 + core
    twin = x_lo * 32 + z * 2 + (1 - core)

    peers = []
    for dz in (8, 9, 7, 10, 6, 11, 5, 12, 4, 13, 3, 14, 2, 15, 1, 0):
        for dx, dc in ((1, 0), (1, 1), (0, 0), (0, 1)):
            if (dz, dx, dc) != (0, 0, 0):
                peers.append(((x_lo + dx) % 2) * 32 + ((z + dz) % ZLEN) * 2 + (core + dc) % 2)

    def remote(src, dst, ss, rs, **where):
        return pltpu.make_async_remote_copy(
            src_ref=src, dst_ref=dst, send_sem=ss, recv_sem=rs, device_id=where, device_id_type=MESH
        )

    fetches = [
        pltpu.make_async_copy(src, dst, fetch_s.at[i])
        for i, (src, dst) in enumerate(
            [
                (k_hbm, k_ref), (v_hbm, v_ref), (t_hbm, t_ref), (w_hbm, w_ref), (first_hbm, first_f),
                (second_hbm, second_f), (last_hbm, last_f), (twist_hbm, twist_ref), (q_hbm, q_ref), (skip_hbm, skip_ref),
            ]
        )
    ]
    for fetch in fetches:
        fetch.start()

    barrier = pltpu.get_barrier_semaphore()

    for there in peers:
        pl.semaphore_signal(barrier, inc=1, device_id={"seq": there}, device_id_type=MESH)
    column = [((y + dy) % 4) * 2 + x_hi for dy in (1, 3, 2)]
    beside = y * 2 + (1 - x_hi)
    for other in column + [beside]:
        pl.semaphore_signal(barrier, inc=1, device_id={"chan": other}, device_id_type=MESH)

    for fetch in fetches[:3]:
        fetch.wait()
    signal = k_ref[...].astype(F32) * v_ref[...].astype(F32)
    send_in[...] = jnp.concatenate(
        [signal.T.reshape(SEQ, OWN, ROWS), t_ref[...].T.reshape(SEQ, OWN, ROWS)], axis=1
    ).astype(BF16)
    fetches[3].wait()
    weight[ring, 0] = w_ref[...]
    pl.semaphore_wait(barrier, SEQ - 1 + 4)

    def exchange(source, target, ss, rs, part):
        for there in part:
            remote(source.at[there], target.at[me], ss, rs, seq=there).start()

    def drain(buffer, sem):
        view = buffer.at[pl.ds(0, SEQ - 1)]
        pltpu.make_async_copy(view, view, sem).wait()

    def up_copy(t):
        return remote(weight.at[ring, (ZLEN - t) % ZLEN], weight.at[ring, 15 - t], up_s.at[t], up_r.at[t], seq=up)

    def down_copy(t):
        return remote(weight.at[ring, t], weight.at[ring, t + 1], down_s.at[t], down_r.at[t], seq=down)

    other_ring = (1 - x_lo) * 2 + core

    def part(r, i, count=2):
        return weight.at[r, pl.ds(PAIRS[i], count)]

    def x_copy(i):
        count = 2 if i < 6 else 1
        return remote(part(ring, i, count), part(ring, i, count), x_s.at[i], x_r.at[i], seq=across)

    def core_copy(i):
        return remote(part(ring, i), part(ring, i), core_s.at[i], core_r.at[i], seq=twin)

    def core2_copy(i):
        return remote(part(other_ring, i), part(other_ring, i), core2_s.at[i], core2_r.at[i], seq=twin)

    def far_copy(i):
        src, dst, there = ((10, 9, up), (6, 7, down), (9, 8, up))[i]
        return remote(weight.at[other_ring, src], weight.at[other_ring, dst], far_s.at[i], far_r.at[i], seq=there)

    def ring_step(t):
        up_copy(t).wait_recv()
        if t < 7:
            up_copy(t + 1).start()
            down_copy(t).wait_recv()
            if t < 6:
                down_copy(t + 1).start()
        if t < 6:
            x_copy(t).start()
        if t == 5:
            x_copy(6).start()
        core_copy(t).start()

    def pass_on(i):
        if i < 6:
            x_copy(i).wait_recv()
        if i == 5:
            far_copy(0).start()
            x_copy(6).wait_recv()
            far_copy(1).start()
        if i == 6:
            far_copy(0).wait_recv()
            far_copy(2).start()
            far_copy(1).wait_recv()
        if i == 7:
            far_copy(2).wait_recv()
        core2_copy(i).start()

    up_copy(0).start()
    down_copy(0).start()
    exchange(send_in, recv_in, in_s, in_r, peers[:16])
    ring_step(0)
    exchange(send_in, recv_in, in_s, in_r, peers[16:32])
    ring_step(1)
    exchange(send_in, recv_in, in_s, in_r, peers[32:48])
    pass_on(0)
    exchange(send_in, recv_in, in_s, in_r, peers[48:])
    recv_in[me] = send_in[me]
    for fetch in fetches[4:]:
        fetch.wait()
    first_ref[...] = first_f[...].astype(BF16)
    last_ref[...] = last_f[...].astype(BF16)
    for i in range(2):
        second_ref[2 * i], second_ref[2 * i + 1] = halves(second_f[i])
    cos, sin = twist_ref[0], twist_ref[1]

    ring_step(2)
    pass_on(1)
    drain(recv_in, in_r)
    wide[...] = recv_in[...].astype(F32).reshape(SEQ * 16, ROWS)
    stacked = jnp.concatenate([wide[pl.ds(c, SEQ, stride=16), :] for c in range(16)], axis=1).astype(BF16)
    freq[...] = dot(first_ref[...], jnp.concatenate([stacked, stacked], axis=0))
    for c in range(16):
        cols = pl.ds(c * ROWS, ROWS)
        rows = pl.ds(c * SEQ, SEQ)
        re, im = freq[0:SEQ, cols], freq[SEQ : 2 * SEQ, cols]
        turned = jnp.concatenate([re * cos + im * sin, im * cos - re * sin], axis=1)
        spread_hi[rows, :], spread_lo[rows, :] = halves(turned)
    ring_step(3)
    pass_on(2)
    hi, lo = spread_hi[...], spread_lo[...]
    spec = dot(hi, second_ref[0]) + dot(lo, second_ref[0]) + dot(hi, second_ref[1])
    n = OWN * SEQ
    sr, si, hr, hi_ = spec[:n, :ROWS], spec[:n, ROWS:], spec[n:, :ROWS], spec[n:, ROWS:]
    prod = jnp.concatenate([sr * hr - si * hi_, sr * hi_ + si * hr], axis=1)
    hi, lo = halves(prod)
    back = dot(hi, second_ref[2]) + dot(lo, second_ref[2]) + dot(hi, second_ref[3])
    ring_step(4)
    pass_on(3)
    pieces_hi, pieces_lo = [], []
    for c in range(OWN):
        re, im = back[c * SEQ : (c + 1) * SEQ, :ROWS], back[c * SEQ : (c + 1) * SEQ, ROWS:]
        unturned = jnp.concatenate([re * cos - im * sin, im * cos + re * sin], axis=0)
        hi, lo = halves(unturned)
        pieces_hi.append(hi)
        pieces_lo.append(lo)
    u_hi, u_lo = jnp.concatenate(pieces_hi, axis=1), jnp.concatenate(pieces_lo, axis=1)
    done = dot(last_ref[...], jnp.concatenate([u_hi, u_hi, u_lo], axis=0))
    for c in range(OWN):
        back_f[pl.ds(c, SEQ, stride=OWN), :] = done[:, c * ROWS : (c + 1) * ROWS]
    send_back[...] = back_f[...].reshape(SEQ, OWN, ROWS).astype(BF16)

    exchange(send_back, recv_back, back_s, back_r, peers[:16])
    exchange(send_back, recv_back, back_s, back_r, peers[16:32])
    exchange(send_back, recv_back, back_s, back_r, peers[32:])
    ring_step(5)
    pass_on(4)
    recv_back[me] = send_back[me]
    drain(recv_back, back_r)

    pass_on(5)
    ring_step(6)
    half_slab = SLAB // 2

    def g_copy(source, half, i, other):
        return remote(gated.at[source, half], gated.at[source, half], ga_s.at[i], ga_r.at[i], chan=other)

    sends = []

    def g_send(*what):
        copy = g_copy(*what)
        copy.start()
        sends.append(copy)

    for half in range(2):
        cols = pl.ds(half * half_slab, half_slab)
        devs = pl.ds(half * (SEQ // 2), SEQ // 2)
        convolved = recv_back[devs].astype(F32).reshape(half_slab, ROWS).T
        conv_ref[:, cols] = convolved
        signal = k_ref[:, cols].astype(F32) * v_ref[:, cols].astype(F32)
        mixed_sum = convolved + skip_ref[cols][None, :] * signal
        gated[slab, half] = (q_ref[:, cols].astype(F32) * mixed_sum).astype(BF16)
        if half == 0:
            g_send(slab, 0, 0, beside)
        else:
            for i in range(3):
                g_send(slab, 1, 7 + i, column[i])
            g_send(slab, 1, 10, beside)
            for i in range(3):
                g_send(slab, 0, 1 + i, column[i])
    back_y = [((y + 4 - dy) % 4) * 2 + x_hi for dy in (1, 3, 2)]
    beyond = [((y + 4 - dy) % 4) * 2 + (1 - x_hi) for dy in (1, 3, 2)]
    pass_on(6)
    g_copy(beside, 0, 0, beside).wait_recv()
    for i in range(3):
        g_send(beside, 0, 4 + i, column[i])
    for i in range(3):
        g_copy(back_y[i], 1, 7 + i, column[i]).wait_recv()
        g_send(back_y[i], 1, 11 + i, beside)
    ring_step(7)
    pass_on(7)
    for i in range(8):
        core_copy(i).wait_recv()
        core2_copy(i).wait_recv()

    def term(source, half):
        blocks = []
        for j in range(2):
            rel = (4 * (source % 4) + 2 * half + j + ZLEN - z) % ZLEN
            for c in (0, 1):
                blocks.append(weight[(source // 4) * 2 + c, rel])
        return dot(gated[source, half], jnp.concatenate(blocks, axis=0))

    total = term(slab, 0) + term(slab, 1) + term(beside, 0)
    for i in range(3):
        total = total + term(back_y[i], 1)
    for i in range(3):
        g_copy(back_y[i], 0, 1 + i, column[i]).wait_recv()
        total = total + term(back_y[i], 0)
    g_copy(beside, 1, 10, beside).wait_recv()
    total = total + term(beside, 1)
    for i in range(3):
        g_copy(beyond[i], 0, 4 + i, column[i]).wait_recv()
        total = total + term(beyond[i], 0)
        g_copy(beyond[i], 1, 11 + i, beside).wait_recv()
        total = total + term(beyond[i], 1)
    out_ref[...] = total.astype(BF16)

    drain(send_in, in_s)
    drain(send_back, back_s)
    for t in range(8):
        up_copy(t).wait_send()
        if t < 7:
            down_copy(t).wait_send()
    for i in range(3):
        far_copy(i).wait_send()
    for i in range(8):
        if i < 7:
            x_copy(i).wait_send()
        core_copy(i).wait_send()
        core2_copy(i).wait_send()
    for copy in sends:
        copy.wait_send()


def body(query_proj, key_proj, value_proj, filter_taps, skip_bias, out_weight):
    dma = pltpu.SemaphoreType.DMA
    vmem = pl.BlockSpec(memory_space=pltpu.VMEM)
    consts = [jnp.asarray(t) for t in tables()]
    return pl.pallas_call(
        kernel,
        out_shape=(
            jax.ShapeDtypeStruct((ROWS, SLAB), BF16),
            jax.ShapeDtypeStruct((ROWS, SLAB), F32),
        ),
        in_specs=[pl.BlockSpec(memory_space=pltpu.HBM)] * 10,
        out_specs=(vmem, vmem),
        scratch_shapes=[
            pltpu.VMEM((ROWS, SLAB), BF16),
            pltpu.VMEM((ROWS, SLAB), BF16),
            pltpu.VMEM((ROWS, SLAB), BF16),
            pltpu.VMEM((ROWS, SLAB), F32),
            pltpu.VMEM((SLAB,), F32),
            pltpu.VMEM((WROWS, SLAB), BF16),
            pltpu.VMEM((2 * SEQ, 2 * SEQ), F32),
            pltpu.VMEM((2, 2 * ROWS, 2 * ROWS), F32),
            pltpu.VMEM((SEQ, 6 * SEQ), F32),
            pltpu.VMEM((2, SEQ, ROWS), F32),
            pltpu.VMEM((2 * SEQ, 2 * SEQ), BF16),
            pltpu.VMEM((4, 2 * ROWS, 2 * ROWS), BF16),
            pltpu.VMEM((SEQ, 6 * SEQ), BF16),
            pltpu.VMEM((SEQ, 16, ROWS), BF16),
            pltpu.VMEM((SEQ, 16, ROWS), BF16),
            pltpu.VMEM((SEQ, OWN, ROWS), BF16),
            pltpu.VMEM((SEQ, OWN, ROWS), BF16),
            pltpu.VMEM((SEQ * 16, ROWS), F32),
            pltpu.VMEM((2 * SEQ, 16 * ROWS), F32),
            pltpu.VMEM((16 * SEQ, 2 * ROWS), BF16),
            pltpu.VMEM((16 * SEQ, 2 * ROWS), BF16),
            pltpu.VMEM((SEQ * OWN, ROWS), F32),
            pltpu.VMEM((CHAN, 2, ROWS, SLAB // 2), BF16),
            pltpu.VMEM((4, ZLEN, WROWS, SLAB), BF16),
            dma, dma, dma, dma,
            dma((8,)), dma((8,)), dma((7,)), dma((7,)),
            dma((7,)), dma((7,)), dma((8,)), dma((8,)), dma((8,)), dma((8,)),
            dma((3,)), dma((3,)),
            dma((14,)), dma((14,)), dma((10,)),
        ],
        compiler_params=pltpu.CompilerParams(
            collective_id=0, has_side_effects=True, vmem_limit_bytes=48 * 1024 * 1024
        ),
        name="hyena",
    )(*[pltpu.with_memory_space_constraint(a, pltpu.HBM) for a in (query_proj, key_proj, value_proj, filter_taps, skip_bias, out_weight, *consts)])


def solution(mesh):
    return jax.shard_map(
        body,
        mesh=mesh,
        in_specs=(
            P("seq", "chan"),
            P("seq", "chan"),
            P("seq", "chan"),
            P("seq", "chan"),
            P("chan"),
            P("seq", "chan"),
        ),
        out_specs=(P("seq", "chan"), P("seq", "chan")),
        check_vma=False,
    )
```

```python
import functools
import math

import jax
import jax.numpy as jnp
import ml_dtypes
import numpy as np
from jax import lax
from jax.experimental import pallas as pl
from jax.experimental.pallas import tpu as pltpu
from jax.sharding import PartitionSpec as P

MESH = pl.DeviceIdType.MESH
BF16 = jnp.bfloat16
F32 = jnp.float32

SEQ = 64
ZLEN = 16
CHAN = 8
ROWS = 128
SLAB = 512
OWN = 8
WROWS = 64
SUB = 4
PAIRS = (0, 14, 2, 12, 4, 10, 6, 8)


def split(a):
    hi = a.astype(ml_dtypes.bfloat16)
    lo = (a - hi.astype(np.float64)).astype(ml_dtypes.bfloat16)
    return hi, lo


def tables():
    length = 2 * SEQ * ROWS
    half = np.arange(SEQ) + 0.5
    angle = 2.0 * math.pi / (2 * SEQ) * np.outer(half, np.arange(SEQ))
    first = np.concatenate([np.cos(angle), -np.sin(angle)], axis=0)
    last = first.T * (2.0 / length)
    twist = 2.0 * math.pi / length * np.outer(half, np.arange(ROWS))
    second = 2.0 * math.pi / ROWS * (np.outer(np.arange(ROWS), np.arange(ROWS)) % ROWS)
    c, s = np.cos(second), np.sin(second)
    forward = np.block([[c, -s], [s, c]])
    backward = np.block([[c, s], [-s, c]])
    f_hi, f_lo = split(first)
    l_hi, l_lo = split(last)
    return tuple(
        table.astype(np.float32)
        for table in (
            np.concatenate([f_hi, f_lo], axis=1),
            np.stack([forward, backward]),
            np.concatenate([l_hi, l_lo, l_hi], axis=1),
            np.stack([np.cos(twist), np.sin(twist)]),
        )
    )


def dot(a, b):
    return jnp.dot(a, b, preferred_element_type=F32)


def halves(a):
    hi = a.astype(BF16)
    return hi, (a - hi.astype(F32)).astype(BF16)


def kernel(
    q_hbm, k_hbm, v_hbm, t_hbm, skip_hbm, w_hbm, first_hbm, second_hbm, last_hbm, twist_hbm,
    out_ref, conv_ref,
    q_ref, k_ref, v_ref, t_ref, skip_ref, w_ref, first_f, second_f, last_f, twist_ref,
    first_ref, second_ref, last_ref,
    send_in, recv_in, send_back, recv_back, wide, freq, spread_hi, spread_lo, back_f, gated, weight,
    in_s, in_r, back_s, back_r, up_s, up_r, down_s, down_r, x_s, x_r, core_s, core_r, core2_s, core2_r,
    far_s, far_r,
    ga_s, ga_r, fetch_s,
):
    me = lax.axis_index("seq")
    slab = lax.axis_index("chan")
    x_lo, z, core = me // 32, (me % 32) // 2, me % 2
    y, x_hi = slab // 2, slab % 2
    ring = x_lo * 2 + core
    up = x_lo * 32 + ((z + 1) % ZLEN) * 2 + core
    down = x_lo * 32 + ((z + ZLEN - 1) % ZLEN) * 2 + core
    across = (1 - x_lo) * 32 + z * 2 + core
    twin = x_lo * 32 + z * 2 + (1 - core)

    peers = []
    for dz in (8, 9, 7, 10, 6, 11, 5, 12, 4, 13, 3, 14, 2, 15, 1, 0):
        for dx, dc in ((1, 0), (1, 1), (0, 0), (0, 1)):
            if (dz, dx, dc) != (0, 0, 0):
                peers.append(((x_lo + dx) % 2) * 32 + ((z + dz) % ZLEN) * 2 + (core + dc) % 2)

    def remote(src, dst, ss, rs, **where):
        return pltpu.make_async_remote_copy(
            src_ref=src, dst_ref=dst, send_sem=ss, recv_sem=rs, device_id=where, device_id_type=MESH
        )

    fetches = [
        pltpu.make_async_copy(src, dst, fetch_s.at[i])
        for i, (src, dst) in enumerate(
            [
                (k_hbm, k_ref), (v_hbm, v_ref), (t_hbm, t_ref), (w_hbm, w_ref), (first_hbm, first_f),
                (second_hbm, second_f), (last_hbm, last_f), (twist_hbm, twist_ref), (q_hbm, q_ref), (skip_hbm, skip_ref),
            ]
        )
    ]
    for fetch in fetches:
        fetch.start()

    barrier = pltpu.get_barrier_semaphore()

    for there in peers:
        pl.semaphore_signal(barrier, inc=1, device_id={"seq": there}, device_id_type=MESH)
    column = [((y + dy) % 4) * 2 + x_hi for dy in (1, 3, 2)]
    beside = y * 2 + (1 - x_hi)
    for other in column + [beside]:
        pl.semaphore_signal(barrier, inc=1, device_id={"chan": other}, device_id_type=MESH)

    for fetch in fetches[:3]:
        fetch.wait()
    signal = k_ref[...].astype(F32) * v_ref[...].astype(F32)
    send_in[...] = jnp.concatenate(
        [signal.T.reshape(SEQ, OWN, ROWS), t_ref[...].T.reshape(SEQ, OWN, ROWS)], axis=1
    ).astype(BF16)
    fetches[3].wait()
    weight[ring, 0] = w_ref[...]
    pl.semaphore_wait(barrier, SEQ - 1 + 4)

    def exchange(source, target, ss, rs, part):
        for there in part:
            remote(source.at[there], target.at[me], ss, rs, seq=there).start()

    def drain(buffer, sem):
        view = buffer.at[pl.ds(0, SEQ - 1)]
        pltpu.make_async_copy(view, view, sem).wait()

    def piece(r, slot, k):
        return weight.at[r, slot, pl.ds(k * (WROWS // SUB), WROWS // SUB)]

    def up_copy(t, k):
        src, dst = piece(ring, (ZLEN - t) % ZLEN, k), piece(ring, 15 - t, k)
        return remote(src, dst, up_s.at[t * SUB + k], up_r.at[t * SUB + k], seq=up)

    def down_copy(t, k):
        src, dst = piece(ring, t, k), piece(ring, t + 1, k)
        return remote(src, dst, down_s.at[t * SUB + k], down_r.at[t * SUB + k], seq=down)

    other_ring = (1 - x_lo) * 2 + core

    def part(r, i, count=2):
        return weight.at[r, pl.ds(PAIRS[i], count)]

    def x_copy(i):
        count = 2 if i < 6 else 1
        return remote(part(ring, i, count), part(ring, i, count), x_s.at[i], x_r.at[i], seq=across)

    def core_copy(i):
        return remote(part(ring, i), part(ring, i), core_s.at[i], core_r.at[i], seq=twin)

    def core2_copy(i):
        return remote(part(other_ring, i), part(other_ring, i), core2_s.at[i], core2_r.at[i], seq=twin)

    def far_copy(i, k):
        src, dst, there = ((10, 9, up), (6, 7, down), (9, 8, up))[i]
        n = i * SUB + k
        return remote(piece(other_ring, src, k), piece(other_ring, dst, k), far_s.at[n], far_r.at[n], seq=there)

    def ring_step(t):
        for k in range(SUB):
            up_copy(t, k).wait_recv()
            if t < 7:
                up_copy(t + 1, k).start()
                down_copy(t, k).wait_recv()
                if t < 6:
                    down_copy(t + 1, k).start()
        if t < 6:
            x_copy(t).start()
        if t == 5:
            x_copy(6).start()
        core_copy(t).start()

    def pass_on(i):
        if i < 6:
            x_copy(i).wait_recv()
        if i == 5:
            for k in range(SUB):
                far_copy(0, k).start()
            x_copy(6).wait_recv()
            for k in range(SUB):
                far_copy(1, k).start()
        if i == 6:
            for k in range(SUB):
                far_copy(0, k).wait_recv()
                far_copy(2, k).start()
            for k in range(SUB):
                far_copy(1, k).wait_recv()
        if i == 7:
            for k in range(SUB):
                far_copy(2, k).wait_recv()
        core2_copy(i).start()

    for k in range(SUB):
        up_copy(0, k).start()
        down_copy(0, k).start()
    exchange(send_in, recv_in, in_s, in_r, peers[:16])
    ring_step(0)
    exchange(send_in, recv_in, in_s, in_r, peers[16:32])
    ring_step(1)
    exchange(send_in, recv_in, in_s, in_r, peers[32:48])
    pass_on(0)
    exchange(send_in, recv_in, in_s, in_r, peers[48:])
    recv_in[me] = send_in[me]
    for fetch in fetches[4:]:
        fetch.wait()
    first_ref[...] = first_f[...].astype(BF16)
    last_ref[...] = last_f[...].astype(BF16)
    for i in range(2):
        second_ref[2 * i], second_ref[2 * i + 1] = halves(second_f[i])
    cos, sin = twist_ref[0], twist_ref[1]

    ring_step(2)
    pass_on(1)
    drain(recv_in, in_r)
    wide[...] = recv_in[...].astype(F32).reshape(SEQ * 16, ROWS)
    stacked = jnp.concatenate([wide[pl.ds(c, SEQ, stride=16), :] for c in range(16)], axis=1).astype(BF16)
    freq[...] = dot(first_ref[...], jnp.concatenate([stacked, stacked], axis=0))
    for c in range(16):
        cols = pl.ds(c * ROWS, ROWS)
        rows = pl.ds(c * SEQ, SEQ)
        re, im = freq[0:SEQ, cols], freq[SEQ : 2 * SEQ, cols]
        turned = jnp.concatenate([re * cos + im * sin, im * cos - re * sin], axis=1)
        spread_hi[rows, :], spread_lo[rows, :] = halves(turned)
    ring_step(3)
    pass_on(2)
    hi, lo = spread_hi[...], spread_lo[...]
    spec = dot(hi, second_ref[0]) + dot(lo, second_ref[0]) + dot(hi, second_ref[1])
    n = OWN * SEQ
    sr, si, hr, hi_ = spec[:n, :ROWS], spec[:n, ROWS:], spec[n:, :ROWS], spec[n:, ROWS:]
    prod = jnp.concatenate([sr * hr - si * hi_, sr * hi_ + si * hr], axis=1)
    hi, lo = halves(prod)
    back = dot(hi, second_ref[2]) + dot(lo, second_ref[2]) + dot(hi, second_ref[3])
    ring_step(4)
    pass_on(3)
    pieces_hi, pieces_lo = [], []
    for c in range(OWN):
        re, im = back[c * SEQ : (c + 1) * SEQ, :ROWS], back[c * SEQ : (c + 1) * SEQ, ROWS:]
        unturned = jnp.concatenate([re * cos - im * sin, im * cos + re * sin], axis=0)
        hi, lo = halves(unturned)
        pieces_hi.append(hi)
        pieces_lo.append(lo)
    u_hi, u_lo = jnp.concatenate(pieces_hi, axis=1), jnp.concatenate(pieces_lo, axis=1)
    done = dot(last_ref[...], jnp.concatenate([u_hi, u_hi, u_lo], axis=0))
    for c in range(OWN):
        back_f[pl.ds(c, SEQ, stride=OWN), :] = done[:, c * ROWS : (c + 1) * ROWS]
    send_back[...] = back_f[...].reshape(SEQ, OWN, ROWS).astype(BF16)

    exchange(send_back, recv_back, back_s, back_r, peers[:16])
    exchange(send_back, recv_back, back_s, back_r, peers[16:32])
    exchange(send_back, recv_back, back_s, back_r, peers[32:])
    ring_step(5)
    pass_on(4)
    recv_back[me] = send_back[me]
    drain(recv_back, back_r)

    pass_on(5)
    ring_step(6)
    half_slab = SLAB // 2

    def g_copy(source, half, i, other):
        return remote(gated.at[source, half], gated.at[source, half], ga_s.at[i], ga_r.at[i], chan=other)

    sends = []

    def g_send(*what):
        copy = g_copy(*what)
        copy.start()
        sends.append(copy)

    for half in range(2):
        cols = pl.ds(half * half_slab, half_slab)
        devs = pl.ds(half * (SEQ // 2), SEQ // 2)
        convolved = recv_back[devs].astype(F32).reshape(half_slab, ROWS).T
        conv_ref[:, cols] = convolved
        signal = k_ref[:, cols].astype(F32) * v_ref[:, cols].astype(F32)
        mixed_sum = convolved + skip_ref[cols][None, :] * signal
        gated[slab, half] = (q_ref[:, cols].astype(F32) * mixed_sum).astype(BF16)
        if half == 0:
            g_send(slab, 0, 0, beside)
        else:
            for i in range(3):
                g_send(slab, 1, 7 + i, column[i])
            g_send(slab, 1, 10, beside)
            for i in range(3):
                g_send(slab, 0, 1 + i, column[i])
    back_y = [((y + 4 - dy) % 4) * 2 + x_hi for dy in (1, 3, 2)]
    beyond = [((y + 4 - dy) % 4) * 2 + (1 - x_hi) for dy in (1, 3, 2)]
    pass_on(6)
    g_copy(beside, 0, 0, beside).wait_recv()
    for i in range(3):
        g_send(beside, 0, 4 + i, column[i])
    for i in range(3):
        g_copy(back_y[i], 1, 7 + i, column[i]).wait_recv()
        g_send(back_y[i], 1, 11 + i, beside)
    ring_step(7)
    pass_on(7)
    for i in range(8):
        core_copy(i).wait_recv()
        core2_copy(i).wait_recv()

    def term(source, half):
        blocks = []
        for j in range(2):
            rel = (4 * (source % 4) + 2 * half + j + ZLEN - z) % ZLEN
            for c in (0, 1):
                blocks.append(weight[(source // 4) * 2 + c, rel])
        return dot(gated[source, half], jnp.concatenate(blocks, axis=0))

    total = term(slab, 0) + term(slab, 1) + term(beside, 0)
    for i in range(3):
        total = total + term(back_y[i], 1)
    for i in range(3):
        g_copy(back_y[i], 0, 1 + i, column[i]).wait_recv()
        total = total + term(back_y[i], 0)
    g_copy(beside, 1, 10, beside).wait_recv()
    total = total + term(beside, 1)
    for i in range(3):
        g_copy(beyond[i], 0, 4 + i, column[i]).wait_recv()
        total = total + term(beyond[i], 0)
        g_copy(beyond[i], 1, 11 + i, beside).wait_recv()
        total = total + term(beyond[i], 1)
    out_ref[...] = total.astype(BF16)

    drain(send_in, in_s)
    drain(send_back, back_s)
    for k in range(SUB):
        for t in range(8):
            up_copy(t, k).wait_send()
            if t < 7:
                down_copy(t, k).wait_send()
        for i in range(3):
            far_copy(i, k).wait_send()
    for i in range(8):
        if i < 7:
            x_copy(i).wait_send()
        core_copy(i).wait_send()
        core2_copy(i).wait_send()
    for copy in sends:
        copy.wait_send()


def body(query_proj, key_proj, value_proj, filter_taps, skip_bias, out_weight):
    dma = pltpu.SemaphoreType.DMA
    vmem = pl.BlockSpec(memory_space=pltpu.VMEM)
    consts = [jnp.asarray(t) for t in tables()]
    return pl.pallas_call(
        kernel,
        out_shape=(
            jax.ShapeDtypeStruct((ROWS, SLAB), BF16),
            jax.ShapeDtypeStruct((ROWS, SLAB), F32),
        ),
        in_specs=[pl.BlockSpec(memory_space=pltpu.HBM)] * 10,
        out_specs=(vmem, vmem),
        scratch_shapes=[
            pltpu.VMEM((ROWS, SLAB), BF16),
            pltpu.VMEM((ROWS, SLAB), BF16),
            pltpu.VMEM((ROWS, SLAB), BF16),
            pltpu.VMEM((ROWS, SLAB), F32),
            pltpu.VMEM((SLAB,), F32),
            pltpu.VMEM((WROWS, SLAB), BF16),
            pltpu.VMEM((2 * SEQ, 2 * SEQ), F32),
            pltpu.VMEM((2, 2 * ROWS, 2 * ROWS), F32),
            pltpu.VMEM((SEQ, 6 * SEQ), F32),
            pltpu.VMEM((2, SEQ, ROWS), F32),
            pltpu.VMEM((2 * SEQ, 2 * SEQ), BF16),
            pltpu.VMEM((4, 2 * ROWS, 2 * ROWS), BF16),
            pltpu.VMEM((SEQ, 6 * SEQ), BF16),
            pltpu.VMEM((SEQ, 16, ROWS), BF16),
            pltpu.VMEM((SEQ, 16, ROWS), BF16),
            pltpu.VMEM((SEQ, OWN, ROWS), BF16),
            pltpu.VMEM((SEQ, OWN, ROWS), BF16),
            pltpu.VMEM((SEQ * 16, ROWS), F32),
            pltpu.VMEM((2 * SEQ, 16 * ROWS), F32),
            pltpu.VMEM((16 * SEQ, 2 * ROWS), BF16),
            pltpu.VMEM((16 * SEQ, 2 * ROWS), BF16),
            pltpu.VMEM((SEQ * OWN, ROWS), F32),
            pltpu.VMEM((CHAN, 2, ROWS, SLAB // 2), BF16),
            pltpu.VMEM((4, ZLEN, WROWS, SLAB), BF16),
            dma, dma, dma, dma,
            dma((8 * SUB,)), dma((8 * SUB,)), dma((7 * SUB,)), dma((7 * SUB,)),
            dma((7,)), dma((7,)), dma((8,)), dma((8,)), dma((8,)), dma((8,)),
            dma((3 * SUB,)), dma((3 * SUB,)),
            dma((14,)), dma((14,)), dma((10,)),
        ],
        compiler_params=pltpu.CompilerParams(
            collective_id=0, has_side_effects=True, vmem_limit_bytes=48 * 1024 * 1024
        ),
        name="hyena",
    )(*[pltpu.with_memory_space_constraint(a, pltpu.HBM) for a in (query_proj, key_proj, value_proj, filter_taps, skip_bias, out_weight, *consts)])


def solution(mesh):
    return jax.shard_map(
        body,
        mesh=mesh,
        in_specs=(
            P("seq", "chan"),
            P("seq", "chan"),
            P("seq", "chan"),
            P("seq", "chan"),
            P("chan"),
            P("seq", "chan"),
        ),
        out_specs=(P("seq", "chan"), P("seq", "chan")),
        check_vma=False,
    )
```

```python
import functools
import math

import jax
import jax.numpy as jnp
import ml_dtypes
import numpy as np
from jax import lax
from jax.experimental import pallas as pl
from jax.experimental.pallas import tpu as pltpu
from jax.sharding import PartitionSpec as P

MESH = pl.DeviceIdType.MESH
BF16 = jnp.bfloat16
F32 = jnp.float32

SEQ = 64
ZLEN = 16
CHAN = 8
ROWS = 128
SLAB = 512
OWN = 8
WROWS = 64
SUB = 4
PAIRS = (0, 14, 2, 12, 4, 10, 6, 8)


def split(a):
    hi = a.astype(ml_dtypes.bfloat16)
    lo = (a - hi.astype(np.float64)).astype(ml_dtypes.bfloat16)
    return hi, lo


def tables():
    length = 2 * SEQ * ROWS
    half = np.arange(SEQ) + 0.5
    angle = 2.0 * math.pi / (2 * SEQ) * np.outer(half, np.arange(SEQ))
    first = np.concatenate([np.cos(angle), -np.sin(angle)], axis=0)
    last = first.T * (2.0 / length)
    twist = 2.0 * math.pi / length * np.outer(half, np.arange(ROWS))
    second = 2.0 * math.pi / ROWS * (np.outer(np.arange(ROWS), np.arange(ROWS)) % ROWS)
    c, s = np.cos(second), np.sin(second)
    forward = np.block([[c, -s], [s, c]])
    backward = np.block([[c, s], [-s, c]])
    f_hi, f_lo = split(first)
    l_hi, l_lo = split(last)
    return tuple(
        table.astype(np.float32)
        for table in (
            np.concatenate([f_hi, f_lo], axis=1),
            np.stack([forward, backward]),
            np.concatenate([l_hi, l_lo, l_hi], axis=1),
            np.stack([np.cos(twist), np.sin(twist)]),
        )
    )


def dot(a, b):
    return jnp.dot(a, b, preferred_element_type=F32)


def halves(a):
    hi = a.astype(BF16)
    return hi, (a - hi.astype(F32)).astype(BF16)


def kernel(
    q_hbm, k_hbm, v_hbm, t_hbm, skip_hbm, w_hbm, first_hbm, second_hbm, last_hbm, twist_hbm,
    out_ref, conv_ref,
    q_ref, k_ref, v_ref, t_ref, skip_ref, w_ref, first_f, second_f, last_f, twist_ref,
    first_ref, second_ref, last_ref,
    send_in, recv_in, send_back, recv_back, wide, freq, spread_hi, spread_lo, back_f, gated, weight,
    in_s, in_r, back_s, back_r, up_s, up_r, down_s, down_r, x_s, x_r, core_s, core_r, core2_s, core2_r,
    far_s, far_r,
    ga_s, ga_r, fetch_s,
):
    me = lax.axis_index("seq")
    slab = lax.axis_index("chan")
    x_lo, z, core = me // 32, (me % 32) // 2, me % 2
    y, x_hi = slab // 2, slab % 2
    ring = x_lo * 2 + core
    up = x_lo * 32 + ((z + 1) % ZLEN) * 2 + core
    down = x_lo * 32 + ((z + ZLEN - 1) % ZLEN) * 2 + core
    across = (1 - x_lo) * 32 + z * 2 + core
    twin = x_lo * 32 + z * 2 + (1 - core)

    peers = []
    for dz in (8, 9, 7, 10, 6, 11, 5, 12, 4, 13, 3, 14, 2, 15, 1, 0):
        for dx, dc in ((1, 0), (1, 1), (0, 0), (0, 1)):
            if (dz, dx, dc) != (0, 0, 0):
                peers.append(((x_lo + dx) % 2) * 32 + ((z + dz) % ZLEN) * 2 + (core + dc) % 2)

    def remote(src, dst, ss, rs, **where):
        return pltpu.make_async_remote_copy(
            src_ref=src, dst_ref=dst, send_sem=ss, recv_sem=rs, device_id=where, device_id_type=MESH
        )

    fetches = [
        pltpu.make_async_copy(src, dst, fetch_s.at[i])
        for i, (src, dst) in enumerate(
            [
                (k_hbm, k_ref), (v_hbm, v_ref), (t_hbm, t_ref), (w_hbm, w_ref), (first_hbm, first_f),
                (second_hbm, second_f), (last_hbm, last_f), (twist_hbm, twist_ref), (q_hbm, q_ref), (skip_hbm, skip_ref),
            ]
        )
    ]
    for fetch in fetches:
        fetch.start()

    barrier = pltpu.get_barrier_semaphore()

    for there in peers:
        pl.semaphore_signal(barrier, inc=1, device_id={"seq": there}, device_id_type=MESH)
    column = [((y + dy) % 4) * 2 + x_hi for dy in (1, 3, 2)]
    beside = y * 2 + (1 - x_hi)
    for other in column + [beside]:
        pl.semaphore_signal(barrier, inc=1, device_id={"chan": other}, device_id_type=MESH)

    for fetch in fetches[:3]:
        fetch.wait()
    signal = k_ref[...].astype(F32) * v_ref[...].astype(F32)
    send_in[...] = jnp.concatenate(
        [signal.T.reshape(SEQ, OWN, ROWS), t_ref[...].T.reshape(SEQ, OWN, ROWS)], axis=1
    ).astype(BF16)
    fetches[3].wait()
    weight[ring, 0] = w_ref[...]
    pl.semaphore_wait(barrier, SEQ - 1 + 4)

    def exchange(source, target, ss, rs, part):
        for there in part:
            remote(source.at[there], target.at[me], ss, rs, seq=there).start()

    def drain(buffer, sem):
        view = buffer.at[pl.ds(0, SEQ - 1)]
        pltpu.make_async_copy(view, view, sem).wait()

    def piece(r, slot, k):
        return weight.at[r, slot, pl.ds(k * (WROWS // SUB), WROWS // SUB)]

    def up_copy(t, k):
        src, dst = piece(ring, (ZLEN - t) % ZLEN, k), piece(ring, 15 - t, k)
        return remote(src, dst, up_s.at[t * SUB + k], up_r.at[t * SUB + k], seq=up)

    def down_copy(t, k):
        src, dst = piece(ring, t, k), piece(ring, t + 1, k)
        return remote(src, dst, down_s.at[t * SUB + k], down_r.at[t * SUB + k], seq=down)

    other_ring = (1 - x_lo) * 2 + core

    def part(r, i, count=2):
        return weight.at[r, pl.ds(PAIRS[i], count)]

    def x_copy(i):
        count = 2 if i < 6 else 1
        return remote(part(ring, i, count), part(ring, i, count), x_s.at[i], x_r.at[i], seq=across)

    def core_copy(i):
        return remote(part(ring, i), part(ring, i), core_s.at[i], core_r.at[i], seq=twin)

    def core2_copy(i):
        return remote(part(other_ring, i), part(other_ring, i), core2_s.at[i], core2_r.at[i], seq=twin)

    def far_copy(i, k):
        src, dst, there = ((10, 9, up), (6, 7, down), (9, 8, up))[i]
        n = i * SUB + k
        return remote(piece(other_ring, src, k), piece(other_ring, dst, k), far_s.at[n], far_r.at[n], seq=there)

    def ring_step(t):
        for k in range(SUB):
            up_copy(t, k).wait_recv()
            if t < 7:
                up_copy(t + 1, k).start()
                down_copy(t, k).wait_recv()
                if t < 6:
                    down_copy(t + 1, k).start()
        if t < 6:
            x_copy(t).start()
        if t == 5:
            x_copy(6).start()
        core_copy(t).start()

    def pass_on(i):
        if i < 6:
            x_copy(i).wait_recv()
        if i == 5:
            for k in range(SUB):
                far_copy(0, k).start()
            x_copy(6).wait_recv()
            for k in range(SUB):
                far_copy(1, k).start()
        if i == 6:
            for k in range(SUB):
                far_copy(0, k).wait_recv()
                far_copy(2, k).start()
            for k in range(SUB):
                far_copy(1, k).wait_recv()
        if i == 7:
            for k in range(SUB):
                far_copy(2, k).wait_recv()
        core2_copy(i).start()

    for k in range(SUB):
        up_copy(0, k).start()
        down_copy(0, k).start()
    exchange(send_in, recv_in, in_s, in_r, peers[:16])
    ring_step(0)
    exchange(send_in, recv_in, in_s, in_r, peers[16:32])
    ring_step(1)
    exchange(send_in, recv_in, in_s, in_r, peers[32:48])
    pass_on(0)
    exchange(send_in, recv_in, in_s, in_r, peers[48:])
    recv_in[me] = send_in[me]
    for fetch in fetches[4:]:
        fetch.wait()
    first_ref[...] = first_f[...].astype(BF16)
    last_ref[...] = last_f[...].astype(BF16)
    for i in range(2):
        hi, lo = halves(second_f[i])
        second_ref[i] = jnp.concatenate([hi, hi, lo], axis=0)
    cos, sin = twist_ref[0], twist_ref[1]

    ring_step(2)
    pass_on(1)
    drain(recv_in, in_r)
    wide[...] = recv_in[...].astype(F32).reshape(SEQ * 16, ROWS)
    stacked = jnp.concatenate([wide[pl.ds(c, SEQ, stride=16), :] for c in range(16)], axis=1).astype(BF16)
    freq[...] = dot(first_ref[...], jnp.concatenate([stacked, stacked], axis=0))
    for c in range(16):
        cols = pl.ds(c * ROWS, ROWS)
        rows = pl.ds(c * SEQ, SEQ)
        re, im = freq[0:SEQ, cols], freq[SEQ : 2 * SEQ, cols]
        turned = jnp.concatenate([re * cos + im * sin, im * cos - re * sin], axis=1)
        spread_hi[rows, :], spread_lo[rows, :] = halves(turned)
    ring_step(3)
    pass_on(2)
    hi, lo = spread_hi[...], spread_lo[...]
    spec = dot(jnp.concatenate([hi, lo, hi], axis=1), second_ref[0])
    n = OWN * SEQ
    sr, si, hr, hi_ = spec[:n, :ROWS], spec[:n, ROWS:], spec[n:, :ROWS], spec[n:, ROWS:]
    prod = jnp.concatenate([sr * hr - si * hi_, sr * hi_ + si * hr], axis=1)
    hi, lo = halves(prod)
    back = dot(jnp.concatenate([hi, lo, hi], axis=1), second_ref[1])
    ring_step(4)
    pass_on(3)
    pieces_hi, pieces_lo = [], []
    for c in range(OWN):
        re, im = back[c * SEQ : (c + 1) * SEQ, :ROWS], back[c * SEQ : (c + 1) * SEQ, ROWS:]
        unturned = jnp.concatenate([re * cos - im * sin, im * cos + re * sin], axis=0)
        hi, lo = halves(unturned)
        pieces_hi.append(hi)
        pieces_lo.append(lo)
    u_hi, u_lo = jnp.concatenate(pieces_hi, axis=1), jnp.concatenate(pieces_lo, axis=1)
    done = dot(last_ref[...], jnp.concatenate([u_hi, u_hi, u_lo], axis=0))
    for c in range(OWN):
        back_f[pl.ds(c, SEQ, stride=OWN), :] = done[:, c * ROWS : (c + 1) * ROWS]
    send_back[...] = back_f[...].reshape(SEQ, OWN, ROWS).astype(BF16)

    exchange(send_back, recv_back, back_s, back_r, peers[:16])
    exchange(send_back, recv_back, back_s, back_r, peers[16:32])
    exchange(send_back, recv_back, back_s, back_r, peers[32:])
    ring_step(5)
    pass_on(4)
    recv_back[me] = send_back[me]
    drain(recv_back, back_r)

    pass_on(5)
    ring_step(6)
    half_slab = SLAB // 2

    def g_copy(source, half, i, other):
        return remote(gated.at[source, half], gated.at[source, half], ga_s.at[i], ga_r.at[i], chan=other)

    sends = []

    def g_send(*what):
        copy = g_copy(*what)
        copy.start()
        sends.append(copy)

    for half in range(2):
        cols = pl.ds(half * half_slab, half_slab)
        devs = pl.ds(half * (SEQ // 2), SEQ // 2)
        convolved = recv_back[devs].astype(F32).reshape(half_slab, ROWS).T
        conv_ref[:, cols] = convolved
        signal = k_ref[:, cols].astype(F32) * v_ref[:, cols].astype(F32)
        mixed_sum = convolved + skip_ref[cols][None, :] * signal
        gated[slab, half] = (q_ref[:, cols].astype(F32) * mixed_sum).astype(BF16)
        if half == 0:
            g_send(slab, 0, 0, beside)
        else:
            for i in range(3):
                g_send(slab, 1, 7 + i, column[i])
            g_send(slab, 1, 10, beside)
            for i in range(3):
                g_send(slab, 0, 1 + i, column[i])
    back_y = [((y + 4 - dy) % 4) * 2 + x_hi for dy in (1, 3, 2)]
    beyond = [((y + 4 - dy) % 4) * 2 + (1 - x_hi) for dy in (1, 3, 2)]
    pass_on(6)
    g_copy(beside, 0, 0, beside).wait_recv()
    for i in range(3):
        g_send(beside, 0, 4 + i, column[i])
    for i in range(3):
        g_copy(back_y[i], 1, 7 + i, column[i]).wait_recv()
        g_send(back_y[i], 1, 11 + i, beside)
    ring_step(7)
    pass_on(7)
    for i in range(8):
        core_copy(i).wait_recv()
        core2_copy(i).wait_recv()

    def term(source, half):
        blocks = []
        for j in range(2):
            rel = (4 * (source % 4) + 2 * half + j + ZLEN - z) % ZLEN
            for c in (0, 1):
                blocks.append(weight[(source // 4) * 2 + c, rel])
        return dot(gated[source, half], jnp.concatenate(blocks, axis=0))

    total = term(slab, 0) + term(slab, 1) + term(beside, 0)
    for i in range(3):
        total = total + term(back_y[i], 1)
    for i in range(3):
        g_copy(back_y[i], 0, 1 + i, column[i]).wait_recv()
        total = total + term(back_y[i], 0)
    g_copy(beside, 1, 10, beside).wait_recv()
    total = total + term(beside, 1)
    for i in range(3):
        g_copy(beyond[i], 0, 4 + i, column[i]).wait_recv()
        total = total + term(beyond[i], 0)
        g_copy(beyond[i], 1, 11 + i, beside).wait_recv()
        total = total + term(beyond[i], 1)
    out_ref[...] = total.astype(BF16)

    drain(send_in, in_s)
    drain(send_back, back_s)
    for k in range(SUB):
        for t in range(8):
            up_copy(t, k).wait_send()
            if t < 7:
                down_copy(t, k).wait_send()
        for i in range(3):
            far_copy(i, k).wait_send()
    for i in range(8):
        if i < 7:
            x_copy(i).wait_send()
        core_copy(i).wait_send()
        core2_copy(i).wait_send()
    for copy in sends:
        copy.wait_send()


def body(query_proj, key_proj, value_proj, filter_taps, skip_bias, out_weight):
    dma = pltpu.SemaphoreType.DMA
    vmem = pl.BlockSpec(memory_space=pltpu.VMEM)
    consts = [jnp.asarray(t) for t in tables()]
    return pl.pallas_call(
        kernel,
        out_shape=(
            jax.ShapeDtypeStruct((ROWS, SLAB), BF16),
            jax.ShapeDtypeStruct((ROWS, SLAB), F32),
        ),
        in_specs=[pl.BlockSpec(memory_space=pltpu.HBM)] * 10,
        out_specs=(vmem, vmem),
        scratch_shapes=[
            pltpu.VMEM((ROWS, SLAB), BF16),
            pltpu.VMEM((ROWS, SLAB), BF16),
            pltpu.VMEM((ROWS, SLAB), BF16),
            pltpu.VMEM((ROWS, SLAB), F32),
            pltpu.VMEM((SLAB,), F32),
            pltpu.VMEM((WROWS, SLAB), BF16),
            pltpu.VMEM((2 * SEQ, 2 * SEQ), F32),
            pltpu.VMEM((2, 2 * ROWS, 2 * ROWS), F32),
            pltpu.VMEM((SEQ, 6 * SEQ), F32),
            pltpu.VMEM((2, SEQ, ROWS), F32),
            pltpu.VMEM((2 * SEQ, 2 * SEQ), BF16),
            pltpu.VMEM((2, 6 * ROWS, 2 * ROWS), BF16),
            pltpu.VMEM((SEQ, 6 * SEQ), BF16),
            pltpu.VMEM((SEQ, 16, ROWS), BF16),
            pltpu.VMEM((SEQ, 16, ROWS), BF16),
            pltpu.VMEM((SEQ, OWN, ROWS), BF16),
            pltpu.VMEM((SEQ, OWN, ROWS), BF16),
            pltpu.VMEM((SEQ * 16, ROWS), F32),
            pltpu.VMEM((2 * SEQ, 16 * ROWS), F32),
            pltpu.VMEM((16 * SEQ, 2 * ROWS), BF16),
            pltpu.VMEM((16 * SEQ, 2 * ROWS), BF16),
            pltpu.VMEM((SEQ * OWN, ROWS), F32),
            pltpu.VMEM((CHAN, 2, ROWS, SLAB // 2), BF16),
            pltpu.VMEM((4, ZLEN, WROWS, SLAB), BF16),
            dma, dma, dma, dma,
            dma((8 * SUB,)), dma((8 * SUB,)), dma((7 * SUB,)), dma((7 * SUB,)),
            dma((7,)), dma((7,)), dma((8,)), dma((8,)), dma((8,)), dma((8,)),
            dma((3 * SUB,)), dma((3 * SUB,)),
            dma((14,)), dma((14,)), dma((10,)),
        ],
        compiler_params=pltpu.CompilerParams(
            collective_id=0, has_side_effects=True, vmem_limit_bytes=48 * 1024 * 1024
        ),
        name="hyena",
    )(*[pltpu.with_memory_space_constraint(a, pltpu.HBM) for a in (query_proj, key_proj, value_proj, filter_taps, skip_bias, out_weight, *consts)])


def solution(mesh):
    return jax.shard_map(
        body,
        mesh=mesh,
        in_specs=(
            P("seq", "chan"),
            P("seq", "chan"),
            P("seq", "chan"),
            P("seq", "chan"),
            P("chan"),
            P("seq", "chan"),
        ),
        out_specs=(P("seq", "chan"), P("seq", "chan")),
        check_vma=False,
    )
```
